32 devices in a mesh: tile: 2 (over core), lvl: 16 (over z, y, x).
Axes of the slice: x: 2, y: 2, z: 4, core: 2. Of those that a mesh axis runs over, the one named last changes fastest.
Arguments:
- parents: int32 [3, 256, 4], P(None, ('tile', 'lvl')), may hold values from -1 to 767, as said below
- factors: bfloat16 [3, 256, 4, 256, 256], P(None, ('tile', 'lvl')), may hold values from -0.125 to 0.125
- chol: bfloat16 [4, 256, 256, 256], P(None, ('tile', 'lvl')), as said below
- noise: bfloat16 [4, 256, 256, 256], P(None, ('tile', 'lvl')), may hold values from -6 to 6
Outputs:
- samples: bfloat16 [4, 256, 256, 256], P(None, ('tile', 'lvl'))
The draws below stay inside these ranges and needn't reach their ends.
Inputs may be any that keep to these rules, and one draw needn't show every extreme that they name: `parents`: parents of a block of level s + 1 are blocks of levels 0 to s owned by a device of the same spatial tile or of the tile with index one less. Among the 32 entries of one device's blocks of one level, at most 2 name blocks owned by any one device of the same tile and at most 1 name blocks owned by any one device of the previous tile; in every draw, both bounds are reached by some device (devices of tile 0 have no previous tile, so their previous-tile entries are -1). `chol`: lower triangular with a positive diagonal.
All inputs are finite; a program needn't handle non-finite values.
Results may differ from the reference program's by a relative error of at most 0.0032.
Values may be sent and summed in bfloat16 or wider, within the bound.
No kernel may reach another device: no remote copies, remote signals or barrier semaphores. Data moves between devices by JAX's collectives and lax.ppermute only.
A program may use at most 128 MiB of HBM per device.

```python
import jax
import jax.numpy as jnp
from jax import lax

BLOCK = 256
REAL = 256
NPAR = 4
LEVELS = 4
CAP = 2
CAPX = 1
KB = 8
PEERS = 16
NB = 256


def draw_parents(key, part):
    device_count = NB // KB
    ref_count = KB * NPAR
    position_count = PEERS * (CAP + CAPX)

    def one_list(section, device):
        base = jax.random.fold_in(jax.random.fold_in(key, section + 11), device)
        keys = jax.random.split(base, 7)
        own_tile = device // PEERS
        shuffled = jax.random.permutation(keys[0], position_count)
        forced_same = jax.random.randint(keys[1], (), 0, PEERS)
        forced_prior = jax.random.randint(keys[2], (), 0, PEERS)
        positions = jnp.arange(position_count)
        forced = (positions // CAP == forced_same) & (positions < PEERS * CAP) | (positions == PEERS * CAP + forced_prior * CAPX)
        scores = jnp.where(forced, -1, shuffled)
        picked = jnp.argsort(scores, stable=True)[:ref_count]
        picked_forced = forced[picked]
        spread = jax.random.permutation(keys[3], ref_count)
        chosen = picked[spread]
        chosen_forced = picked_forced[spread]
        from_prior = chosen >= PEERS * CAP
        owner_lane = jnp.where(from_prior, (chosen - PEERS * CAP) // CAPX, chosen // CAP)
        owner_tile = own_tile - from_prior.astype(jnp.int32)
        parent_level = jax.random.randint(keys[4], (ref_count,), 0, section + 1)
        within = jax.random.randint(keys[5], (ref_count,), 0, KB)
        dropped = (jax.random.randint(keys[6], (ref_count,), 0, 4) == 0) & jnp.logical_not(chosen_forced)
        usable = (owner_tile >= 0) & jnp.logical_not(dropped)
        block_id = parent_level * NB + (owner_tile * PEERS + owner_lane) * KB + within
        return jnp.where(usable, block_id, -1).astype(jnp.int32).reshape(KB, NPAR)
    lists = jax.vmap(jax.vmap(one_list, (None, 0)), (0, None))(jnp.arange(LEVELS - 1), jnp.arange(device_count))
    return lists.reshape(LEVELS - 1, NB, NPAR)


def draw_chol(key, part):
    key_off, key_diag = jax.random.split(jax.random.fold_in(key, 5))
    off_scale = 0.6
    diag_part = jax.random.uniform(key_diag, (LEVELS, NB, BLOCK), jnp.float32, 0.5, 1.5)
    off_part = jax.random.normal(key_off, (LEVELS, NB, BLOCK, BLOCK), jnp.float32) * (off_scale / BLOCK ** 0.5)
    row_index = jnp.arange(BLOCK)[:, None]
    col_index = jnp.arange(BLOCK)[None, :]
    lower = jnp.where(row_index > col_index, off_part, 0.0)
    diagonal = jnp.where(row_index == col_index, diag_part[..., None], 0.0)
    return (lower + diagonal).astype(jnp.bfloat16)


def shard_levels(rng, shape, pieces, smallest, largest):
    loudness, own = 1.0, jax.random.fold_in(rng, 6)
    for axis_at, parts in pieces:
        steps = jnp.exp(jax.random.uniform(jax.random.fold_in(own, axis_at), (parts,), jnp.float32, smallest / len(pieces), largest / len(pieces)))
        loudness = loudness * jnp.repeat(steps, shape[axis_at] // parts).reshape([-1 if axis == axis_at else 1 for axis in range(len(shape))])
    return loudness


def centred(own_key, shape, width, most, pieces=(), held_as=jnp.bfloat16):
    values = jax.random.normal(own_key, shape, jnp.float32) * width
    if len(pieces) > 0:
        values = shard_levels(own_key, shape, pieces, -0.22, 0.18) * values
    return jnp.clip(values, min=-most, max=most).astype(held_as)


def setup_inputs(seed: int = 0) -> dict:
    key_list = jax.random.split(jax.random.key(seed), 5)
    return {
        "parents": draw_parents(jax.random.fold_in(key_list[4], 71), 0),
        "factors": centred(key_list[1], (LEVELS - 1, NB, NPAR, BLOCK, BLOCK), (8 * BLOCK) ** -0.5, 0.125, ((1, 32),)),
        "chol": draw_chol(jax.random.fold_in(key_list[4], 71), 0),
        "noise": centred(key_list[3], (LEVELS, NB, BLOCK, REAL), 1.0, 6.0, ((1, 32),)),
    }


def reference(parents, factors, chol, noise):
    total_blocks = chol.shape[1]

    def first_block(pair):
        return jnp.dot(pair[0], pair[1], preferred_element_type=jnp.float32).astype(jnp.bfloat16)

    level_zero = lax.map(first_block, (chol[0], noise[0]))
    samples = jnp.zeros((LEVELS, total_blocks, BLOCK, REAL), jnp.bfloat16)
    samples = samples.at[0].set(level_zero)
    for section in range(1, LEVELS):
        flat_samples = samples.reshape(LEVELS * total_blocks, BLOCK, REAL)

        def one_block(items):
            block_ids, amats, lower, draws = items
            total = jnp.dot(lower, draws, preferred_element_type=jnp.float32)
            for slot in range(NPAR):
                where_from = jnp.maximum(block_ids[slot], 0).astype(jnp.int32)
                parent_block = lax.dynamic_index_in_dim(flat_samples, where_from, 0, keepdims=False)
                term = jnp.dot(amats[slot], parent_block, preferred_element_type=jnp.float32)
                total = total + jnp.where(block_ids[slot] >= 0, term, jnp.zeros_like(term))
            return total.astype(jnp.bfloat16)

        level_out = lax.map(one_block, (parents[section - 1], factors[section - 1], chol[section], noise[section]))
        samples = samples.at[section].set(level_out)
    return samples
```

```python
import functools

import jax
import jax.numpy as jnp
from jax import lax
from jax.experimental import pallas as pl
from jax.experimental.pallas import tpu as pltpu
from jax.sharding import PartitionSpec as P

CAP = 2
CAPX = 1
COLS = 4
HALVES = 2
ANY = pl.BlockSpec(memory_space=pl.ANY)


def params(mib):
    return pltpu.CompilerParams(vmem_limit_bytes=mib * 1024 * 1024)


def first_level(chol, noise, out, half):
    depth, blocks, rows, _ = chol.shape
    width = noise.shape[3] // HALVES

    def body(*refs):
        lower, draws, latest, full = refs[0], refs[1], refs[-2], refs[-1]
        value = jnp.dot(lower[0, 0], draws[0, 0], preferred_element_type=jnp.float32)
        value = value.astype(jnp.bfloat16)
        latest[0] = value
        full[0, 0] = value

    carried = [] if out is None else [out]
    return pl.pallas_call(
        body,
        grid=(blocks,),
        in_specs=[
            pl.BlockSpec((1, 1, rows, rows), lambda b: (0, b, 0, 0)),
            pl.BlockSpec((1, 1, rows, width), lambda b: (0, b, 0, half)),
        ]
        + [ANY] * len(carried),
        out_specs=[
            pl.BlockSpec((1, rows, width), lambda b: (b, 0, 0)),
            pl.BlockSpec((1, 1, rows, width), lambda b: (0, b, 0, half)),
        ],
        out_shape=[
            jax.ShapeDtypeStruct((blocks, rows, width), jnp.bfloat16),
            jax.ShapeDtypeStruct(noise.shape, jnp.bfloat16),
        ],
        input_output_aliases={2: 1} if carried else {},
        compiler_params=params(16),
        cost_estimate=pl.CostEstimate(
            flops=2 * blocks * rows * rows * width, bytes_accessed=4_000_000, transcendentals=0
        ),
        name=f"first_{half}",
    )(chol, noise, *carried)


def pick_payload(table, on_middle, fresh, pool, section):
    own, near, mid, far, mid_relay, far_relay = fresh
    blocks, rows, width = own.shape
    same_slots, prior_slots = COLS * CAP, COLS * CAPX
    total = COLS * (same_slots + prior_slots)
    level = section - 1
    has_pool = pool is not None

    def body(tbl, flag, own, near, mid, far, mid_relay, far_relay, *rest):
        rest = rest[1:] if has_pool else rest
        held = rest[0]
        same, prior = rest[1 : 1 + COLS], rest[1 + COLS : 1 + 2 * COLS]
        sems, put_sems = rest[1 + 2 * COLS :]

        def put(source, place):
            return pltpu.make_async_copy(source, held.at[level, place], put_sems.at[place])

        put(own, 0).start()
        put(near, 1).start()

        @pl.when(flag[0] == 1)
        def _():
            put(mid_relay, 2).start()
            put(mid, 3).start()

        @pl.when(flag[0] != 1)
        def _():
            put(far, 2).start()
            put(far_relay, 3).start()

        for place in range(4):
            put(own, place).wait()

        def slot_copy(slot):
            if slot < COLS * same_slots:
                target = same[slot // same_slots].at[slot % same_slots]
            else:
                left = slot - COLS * same_slots
                target = prior[left // prior_slots].at[left % prior_slots]
            where = jnp.maximum(tbl[slot], 0)
            source = held.at[where // (4 * blocks), (where // blocks) % 4, where % blocks]
            return pltpu.make_async_copy(source, target, sems.at[slot])

        for slot in range(total):

            @pl.when(tbl[slot] >= 0)
            def _():
                slot_copy(slot).start()

        for slot in range(total):

            @pl.when(tbl[slot] >= 0)
            def _():
                slot_copy(slot).wait()

    pool_shape = (3, 4, blocks, rows, width)
    carried = [pool] if has_pool else []
    out = pl.pallas_call(
        body,
        in_specs=[pl.BlockSpec(memory_space=pltpu.SMEM)] * 2 + [ANY] * (6 + len(carried)),
        out_specs=[ANY] * (1 + 2 * COLS),
        out_shape=[jax.ShapeDtypeStruct(pool_shape, jnp.bfloat16)]
        + [jax.ShapeDtypeStruct((same_slots, rows, width), jnp.bfloat16)] * COLS
        + [jax.ShapeDtypeStruct((prior_slots, rows, width), jnp.bfloat16)] * COLS,
        scratch_shapes=[pltpu.SemaphoreType.DMA((total,)), pltpu.SemaphoreType.DMA((4,))],
        input_output_aliases={8: 0} if has_pool else {},
        compiler_params=params(16),
        cost_estimate=pl.CostEstimate(flops=0, bytes_accessed=10_000_000, transcendentals=0),
        name=f"pick_{section}",
    )(table, on_middle, *fresh, *carried)
    return out[0], out[1 : 1 + COLS], out[1 + COLS :]


def next_level(places, factors, chol, noise, got, out, section, half):
    depth, blocks, rows, _ = chol.shape
    slots = factors.shape[2]
    width = noise.shape[3] // HALVES
    sizes = [ref.shape[0] for ref in got]
    starts = [sum(sizes[:i]) for i in range(len(sizes))]

    def body(tbl, mats, lower, draws, *rest):
        got = rest[: len(sizes)]
        latest, full, held, sems = rest[len(sizes) + 1 :]
        block = pl.program_id(0)

        def fetch(i):
            return pltpu.make_async_copy(
                got[i], held.at[pl.ds(starts[i], sizes[i])], sems.at[i]
            )

        @pl.when(block == 0)
        def _():
            for i in range(len(sizes)):
                fetch(i).start()

        total = jnp.dot(lower[0, 0], draws[0, 0], preferred_element_type=jnp.float32)

        @pl.when(block == 0)
        def _():
            for i in range(len(sizes)):
                fetch(i).wait()

        for j in range(slots):
            place = tbl[block * slots + j]
            parent = held[jnp.maximum(place, 0)]
            parent = jnp.where(place >= 0, parent, jnp.zeros_like(parent))
            total += jnp.dot(mats[0, 0, j], parent, preferred_element_type=jnp.float32)
        value = total.astype(jnp.bfloat16)
        latest[0] = value
        full[0, 0] = value

    n_got = len(sizes)
    return pl.pallas_call(
        body,
        grid=(blocks,),
        in_specs=[
            pl.BlockSpec(memory_space=pltpu.SMEM),
            pl.BlockSpec((1, 1, slots, rows, rows), lambda b: (section - 1, b, 0, 0, 0)),
            pl.BlockSpec((1, 1, rows, rows), lambda b: (section, b, 0, 0)),
            pl.BlockSpec((1, 1, rows, width), lambda b: (section, b, 0, half)),
        ]
        + [ANY] * (n_got + 1),
        out_specs=[
            pl.BlockSpec((1, rows, width), lambda b: (b, 0, 0)),
            pl.BlockSpec((1, 1, rows, width), lambda b: (section, b, 0, half)),
        ],
        out_shape=[
            jax.ShapeDtypeStruct((blocks, rows, width), jnp.bfloat16),
            jax.ShapeDtypeStruct(noise.shape, jnp.bfloat16),
        ],
        scratch_shapes=[
            pltpu.VMEM((sum(sizes), rows, width), jnp.bfloat16),
            pltpu.SemaphoreType.DMA((n_got,)),
        ],
        input_output_aliases={4 + n_got: 1},
        compiler_params=params(24),
        cost_estimate=pl.CostEstimate(
            flops=2 * (slots + 1) * blocks * rows * rows * width,
            bytes_accessed=10_000_000,
            transcendentals=0,
        ),
        name=f"level_{section}_{half}",
    )(places, factors, chol, noise, *got, out)


def ranks(active, lane):
    count = lane.shape[-1]
    earlier = jnp.arange(count)[:, None] > jnp.arange(count)[None, :]
    alike = (lane[..., :, None] == lane[..., None, :]) & active[..., None, :] & earlier
    return jnp.sum(alike.astype(jnp.int32), axis=-1)


def tables(parents, total_blocks, local_blocks, peer_count, tile_count):
    sections = parents.shape[0]
    own_lane, own_tile = lax.axis_index("lvl"), lax.axis_index("tile")
    own_z, own_col = own_lane // COLS, own_lane % COLS
    mine = parents.reshape(sections, -1)
    onward = lax.ppermute(
        mine,
        "tile",
        [(t + 1, t) for t in range(tile_count - 1)],
    )
    onward = jnp.where(own_tile + 1 < tile_count, onward, -1)
    pair = jnp.stack([mine, onward])
    lists = jnp.stack([pair] + [lax.ppermute(pair, "lvl", across(k, peer_count)) for k in (1, 2, 3)])

    def decode(ids):
        clipped = jnp.maximum(ids, 0)
        level, block = clipped // total_blocks, clipped % total_blocks
        dev = block // local_blocks
        return ids >= 0, level, dev // peer_count, dev % peer_count, block % local_blocks

    valid, level, tile, lane, within = decode(lists)
    active = valid & (tile == own_tile) & (lane % COLS == own_col)
    rank = ranks(active, lane)
    slot = (lane // COLS) * CAP + jnp.minimum(rank, CAP - 1)
    source = (level * 4 + ((lane // COLS) ^ own_z)) * local_blocks + within
    hits = active[..., None] & (slot[..., None] == jnp.arange(COLS * CAP))
    table = jnp.sum(jnp.where(hits, source[..., None] + 1, 0), axis=-2) - 1
    same = table[:, 0]
    prior = table[:, 1, :, ::CAP]
    sends = jnp.concatenate(
        [
            same.transpose(1, 0, 2).reshape(sections, -1),
            prior.transpose(1, 0, 2).reshape(sections, -1),
        ],
        axis=1,
    )
    valid, level, tile, lane, within = decode(mine)
    from_prior = tile != own_tile
    rank = ranks(valid, lane + peer_count * from_prior.astype(jnp.int32))
    apart = (lane % COLS) ^ own_col
    zed = lane // COLS
    place = jnp.where(
        from_prior,
        COLS * COLS * CAP + apart * COLS * CAPX + zed,
        apart * COLS * CAP + zed * CAP + jnp.minimum(rank, CAP - 1),
    )
    return sends, jnp.where(valid, place, -1)


def across(k, peer_count):
    return [(lane, lane ^ k) for lane in range(peer_count)]


def along(links):
    return [(COLS * a + c, COLS * b + c) for a, b in links for c in range(COLS)]


def spread_z(latest):
    send = functools.partial(lax.ppermute, axis_name="lvl")
    near = send(latest, perm=along([(0, 1), (1, 0), (2, 3), (3, 2)]))
    mid = send(latest, perm=along([(1, 2), (2, 1)]))
    mid_relay = send(near, perm=along([(1, 2), (2, 1)]))
    far = send(mid, perm=along([(1, 0), (2, 3)]))
    far_relay = send(mid_relay, perm=along([(1, 0), (2, 3)]))
    return latest, near, mid, far, mid_relay, far_relay


def swap_plane(same, prior, peer_count, tile_count):
    got = [same[0]]
    for k in (1, 2, 3):
        got.append(lax.ppermute(same[k], "lvl", across(k, peer_count)))
    for k in (0, 1, 2, 3):
        links = [
            (t * peer_count + a, (t + 1) * peer_count + b)
            for t in range(tile_count - 1)
            for a, b in across(k, peer_count)
        ]
        got.append(lax.ppermute(prior[k], ("tile", "lvl"), links))
    return got


def shards(parents, factors, chol, noise):
    peer_count = lax.axis_size("lvl")
    tile_count = lax.axis_size("tile")
    depth, local_blocks = chol.shape[:2]
    total_blocks = local_blocks * peer_count * tile_count
    out = None
    latest, pools = [None] * HALVES, [None] * HALVES
    for half in range(HALVES):
        latest[half], out = first_level(chol, noise, out, half)
    sends, places = tables(parents, total_blocks, local_blocks, peer_count, tile_count)
    own_z = lax.axis_index("lvl") // COLS
    on_middle = ((own_z == 1) | (own_z == 2)).astype(jnp.int32).reshape(1)
    for section in range(1, depth):
        for half in range(HALVES):
            fresh = spread_z(latest[half])
            pools[half], same, prior = pick_payload(
                sends[section - 1], on_middle, fresh, pools[half], section
            )
            got = swap_plane(same, prior, peer_count, tile_count)
            latest[half], out = next_level(
                places[section - 1], factors, chol, noise, got, out, section, half
            )
    return out


def solution(mesh):
    placed = (
        P(None, ("tile", "lvl"), None),
        P(None, ("tile", "lvl"), None, None, None),
        P(None, ("tile", "lvl"), None, None),
        P(None, ("tile", "lvl"), None, None),
    )
    return jax.shard_map(
        shards,
        mesh=mesh,
        in_specs=placed,
        out_specs=P(None, ("tile", "lvl"), None, None),
        check_vma=False,
    )
```

```python
import functools

import jax
import jax.numpy as jnp
from jax import lax
from jax.experimental import pallas as pl
from jax.experimental.pallas import tpu as pltpu
from jax.sharding import PartitionSpec as P

CAP = 2
CAPX = 1
COLS = 4
GROUPS = (((0, 1), ()), ((2, 3), (0, 1, 2, 3)))
HALVES = 2
ANY = pl.BlockSpec(memory_space=pl.ANY)


def params(mib):
    return pltpu.CompilerParams(vmem_limit_bytes=mib * 1024 * 1024)


def first_level(chol, noise, out, half, after=()):
    depth, blocks, rows, _ = chol.shape
    width = noise.shape[3] // HALVES

    def body(*refs):
        lower, draws, latest, full = refs[0], refs[1], refs[-2], refs[-1]
        value = jnp.dot(lower[0, 0], draws[0, 0], preferred_element_type=jnp.float32)
        value = value.astype(jnp.bfloat16)
        latest[0] = value
        full[0, 0] = value

    carried = [] if out is None else [out, *after]
    return pl.pallas_call(
        body,
        grid=(blocks,),
        in_specs=[
            pl.BlockSpec((1, 1, rows, rows), lambda b: (0, b, 0, 0)),
            pl.BlockSpec((1, 1, rows, width), lambda b: (0, b, 0, half)),
        ]
        + [ANY] * len(carried),
        out_specs=[
            pl.BlockSpec((1, rows, width), lambda b: (b, 0, 0)),
            pl.BlockSpec((1, 1, rows, width), lambda b: (0, b, 0, half)),
        ],
        out_shape=[
            jax.ShapeDtypeStruct((blocks, rows, width), jnp.bfloat16),
            jax.ShapeDtypeStruct(noise.shape, jnp.bfloat16),
        ],
        input_output_aliases={2: 1} if carried else {},
        compiler_params=params(8),
        cost_estimate=pl.CostEstimate(
            flops=2 * blocks * rows * rows * width, bytes_accessed=4_000_000, transcendentals=0
        ),
        name=f"first_{half}",
    )(chol, noise, *carried)


def pick(table, held, group, name, after=()):
    blocks, rows, width = held[0][0].shape
    ks = sorted(set(group[0] + group[1]))
    same_slots, prior_slots = len(group[0]) * CAP, len(group[1]) * CAPX
    n_same, n_prior = COLS * bool(group[0]), COLS * bool(group[1])
    total = COLS * (same_slots + prior_slots)
    flat = [level[k] for level in held for k in ks]
    count, each, levels = len(flat), len(ks), len(held)

    def body(tbl, *refs):
        held = refs[:count]
        targets = refs[count + len(after) : -1]
        same, prior = targets[:n_same], targets[n_same:]
        sems = refs[-1]

        def slot_copy(slot, source):
            if slot < COLS * same_slots:
                target = same[slot // same_slots].at[slot % same_slots]
            else:
                left = slot - COLS * same_slots
                target = prior[left // prior_slots].at[left % prior_slots]
            return pltpu.make_async_copy(source, target, sems.at[slot])

        for slot in range(total):
            where = tbl[slot]
            if slot < COLS * same_slots:
                k = group[0][slot % same_slots // CAP]
            else:
                k = group[1][(slot - COLS * same_slots) % prior_slots // CAPX]
            at = ks.index(k)
            for level in range(levels):

                @pl.when((where >= level * blocks) & (where < (level + 1) * blocks))
                def _():
                    slot_copy(slot, held[level * each + at].at[where - level * blocks]).start()

        for slot in range(total):

            @pl.when(tbl[slot] >= 0)
            def _():
                slot_copy(slot, held[0].at[0]).wait()

    out = pl.pallas_call(
        body,
        in_specs=[pl.BlockSpec(memory_space=pltpu.SMEM)] + [ANY] * (count + len(after)),
        out_specs=[ANY] * (n_same + n_prior),
        out_shape=[jax.ShapeDtypeStruct((same_slots, rows, width), jnp.bfloat16)] * n_same
        + [jax.ShapeDtypeStruct((prior_slots, rows, width), jnp.bfloat16)] * n_prior,
        scratch_shapes=[pltpu.SemaphoreType.DMA((total,))],
        compiler_params=params(4),
        cost_estimate=pl.CostEstimate(flops=0, bytes_accessed=6_000_000, transcendentals=0),
        name=name,
    )(table, *flat, *after)
    return out[:n_same], out[n_same:]


def next_level(places, factors, chol, noise, got, out, section, half, after=()):
    depth, blocks, rows, _ = chol.shape
    slots = factors.shape[2]
    width = noise.shape[3] // HALVES
    sizes = [ref.shape[0] for ref in got]
    starts = [sum(sizes[:i]) for i in range(len(sizes))]

    def body(tbl, mats, lower, draws, *rest):
        got = rest[: len(sizes)]
        latest, full, held, sems = rest[len(sizes) + 1 + len(after) :]
        block = pl.program_id(0)

        def fetch(i):
            return pltpu.make_async_copy(
                got[i], held.at[pl.ds(starts[i], sizes[i])], sems.at[i]
            )

        @pl.when(block == 0)
        def _():
            for i in range(len(sizes)):
                fetch(i).start()

        total = jnp.dot(lower[0, 0], draws[0, 0], preferred_element_type=jnp.float32)

        @pl.when(block == 0)
        def _():
            for i in range(len(sizes)):
                fetch(i).wait()

        for j in range(slots):
            place = tbl[block * slots + j]
            parent = held[jnp.maximum(place, 0)]
            parent = jnp.where(place >= 0, parent, jnp.zeros_like(parent))
            total += jnp.dot(mats[0, 0, j], parent, preferred_element_type=jnp.float32)
        value = total.astype(jnp.bfloat16)
        latest[0] = value
        full[0, 0] = value

    n_got = len(sizes)
    return pl.pallas_call(
        body,
        grid=(blocks,),
        in_specs=[
            pl.BlockSpec(memory_space=pltpu.SMEM),
            pl.BlockSpec((1, 1, slots, rows, rows), lambda b: (section - 1, b, 0, 0, 0)),
            pl.BlockSpec((1, 1, rows, rows), lambda b: (section, b, 0, 0)),
            pl.BlockSpec((1, 1, rows, width), lambda b: (section, b, 0, half)),
        ]
        + [ANY] * (n_got + 1 + len(after)),
        out_specs=[
            pl.BlockSpec((1, rows, width), lambda b: (b, 0, 0)),
            pl.BlockSpec((1, 1, rows, width), lambda b: (section, b, 0, half)),
        ],
        out_shape=[
            jax.ShapeDtypeStruct((blocks, rows, width), jnp.bfloat16),
            jax.ShapeDtypeStruct(noise.shape, jnp.bfloat16),
        ],
        scratch_shapes=[
            pltpu.VMEM((sum(sizes), rows, width), jnp.bfloat16),
            pltpu.SemaphoreType.DMA((n_got,)),
        ],
        input_output_aliases={4 + n_got: 1},
        compiler_params=params(12),
        cost_estimate=pl.CostEstimate(
            flops=2 * (slots + 1) * blocks * rows * rows * width,
            bytes_accessed=10_000_000,
            transcendentals=0,
        ),
        name=f"level_{section}_{half}",
    )(places, factors, chol, noise, *got, out, *after)


def ranks(active, lane):
    count = lane.shape[-1]
    earlier = jnp.arange(count)[:, None] > jnp.arange(count)[None, :]
    alike = (lane[..., :, None] == lane[..., None, :]) & active[..., None, :] & earlier
    return jnp.sum(alike.astype(jnp.int32), axis=-1)


def tables(parents, total_blocks, local_blocks, peer_count, tile_count):
    sections = parents.shape[0]
    own_lane, own_tile = lax.axis_index("lvl"), lax.axis_index("tile")
    own_z, own_col = own_lane // COLS, own_lane % COLS
    mine = parents.reshape(sections, -1)
    onward = lax.ppermute(
        mine,
        "tile",
        [(t + 1, t) for t in range(tile_count - 1)],
    )
    onward = jnp.where(own_tile + 1 < tile_count, onward, -1)
    pair = jnp.stack([mine, onward])
    lists = jnp.stack([pair] + [lax.ppermute(pair, "lvl", across(k, peer_count)) for k in (1, 2, 3)])

    def decode(ids):
        clipped = jnp.maximum(ids, 0)
        level, block = clipped // total_blocks, clipped % total_blocks
        dev = block // local_blocks
        return ids >= 0, level, dev // peer_count, dev % peer_count, block % local_blocks

    valid, level, tile, lane, within = decode(lists)
    active = valid & (tile == own_tile) & (lane % COLS == own_col)
    rank = jnp.minimum(ranks(active, lane), CAP - 1)
    slot = ((own_z - lane // COLS) % 4) * CAP + rank
    hits = active[..., None] & (slot[..., None] == jnp.arange(4 * CAP))
    source = level * local_blocks + within
    table = jnp.sum(jnp.where(hits, source[..., None] + 1, 0), axis=-2) - 1
    table = table.reshape(COLS, 2, sections, 4, CAP).transpose(1, 2, 0, 3, 4)
    sends = []
    for same_ks, prior_ks in GROUPS:
        same = [table[0, :, c, k] for c in range(COLS) for k in same_ks]
        prior = [table[1, :, c, k, :1] for c in range(COLS) for k in prior_ks]
        sends.append(jnp.concatenate(same + prior, axis=1))

    valid, level, tile, lane, within = decode(mine)
    from_prior = (tile != own_tile).astype(jnp.int32)
    rank = jnp.minimum(ranks(valid, lane + peer_count * from_prior), CAP - 1)
    apart = (lane % COLS) ^ own_col
    ring = (own_z - lane // COLS) % 4
    place, base = jnp.zeros_like(lane), 0
    for same_ks, prior_ks in GROUPS:
        for at, k in enumerate(same_ks):
            slot = base + (apart * len(same_ks) + at) * CAP + rank
            place = jnp.where((ring == k) & (from_prior == 0), slot, place)
        base += COLS * len(same_ks) * CAP
        for at, k in enumerate(prior_ks):
            slot = base + (apart * len(prior_ks) + at) * CAPX
            place = jnp.where((ring == k) & (from_prior == 1), slot, place)
        base += COLS * len(prior_ks) * CAPX
    return sends, jnp.where(valid, place, -1)


def across(k, peer_count):
    return [(lane, lane ^ k) for lane in range(peer_count)]


def ring_z(latest, peer_count):
    links = [(lane, (lane + COLS) % peer_count) for lane in range(peer_count)]
    held = [latest]
    for _ in range(3):
        held.append(lax.ppermute(held[-1], "lvl", links))
    return held


def swap_plane(same, prior, peer_count, tile_count):
    got = list(same[:1])
    for k in range(1, len(same)):
        got.append(lax.ppermute(same[k], "lvl", across(k, peer_count)))
    for k in range(len(prior)):
        links = [
            (t * peer_count + a, (t + 1) * peer_count + b)
            for t in range(tile_count - 1)
            for a, b in across(k, peer_count)
        ]
        got.append(lax.ppermute(prior[k], ("tile", "lvl"), links))
    return got


def shards(parents, factors, chol, noise):
    peer_count = lax.axis_size("lvl")
    tile_count = lax.axis_size("tile")
    depth, local_blocks = chol.shape[:2]
    total_blocks = local_blocks * peer_count * tile_count
    sends, places = tables(parents, total_blocks, local_blocks, peer_count, tile_count)
    held = [[], []]

    def spread(latest, half):
        held[half].append(ring_z(latest, peer_count))
        return held[half][-1]

    def swap(section, half, after=()):
        got = []
        for group, ks in enumerate(GROUPS):
            same, prior = pick(
                sends[group][section], held[half], ks, f"pick_{section}_{half}_{group}", after
            )
            got += swap_plane(same, prior, peer_count, tile_count)
        return got

    lead, out = first_level(chol, noise, None, 0)
    ring = spread(lead, 0)
    lag, out = first_level(chol, noise, out, 1, [ring[1]])
    got = swap(0, 0, [lag])
    ring = spread(lag, 1)
    for section in range(1, depth):
        more = section + 1 < depth
        lead, out = next_level(
            places[section - 1], factors, chol, noise, got, out, section, 0, [ring[2]]
        )
        lag_got = swap(section - 1, 1, [lead])
        ring = spread(lead, 0) if more else None
        lag, out = next_level(
            places[section - 1], factors, chol, noise, lag_got, out, section, 1, [ring[2]] if more else ()
        )
        if more:
            got = swap(section, 0, [lag])
            ring = spread(lag, 1)
    return out


def solution(mesh):
    placed = (
        P(None, ("tile", "lvl"), None),
        P(None, ("tile", "lvl"), None, None, None),
        P(None, ("tile", "lvl"), None, None),
        P(None, ("tile", "lvl"), None, None),
    )
    return jax.shard_map(
        shards,
        mesh=mesh,
        in_specs=placed,
        out_specs=P(None, ("tile", "lvl"), None, None),
        check_vma=False,
    )
```

```python
import functools

import jax
import jax.numpy as jnp
from jax import lax
from jax.experimental import pallas as pl
from jax.experimental.pallas import tpu as pltpu
from jax.sharding import PartitionSpec as P

CAP = 2
CAPX = 1
COLS = 4
GROUPS = (((0, 1), ()), ((2, 3), (0, 1, 2, 3)))
HALVES = 2
ANY = pl.BlockSpec(memory_space=pl.ANY)


def params(mib):
    return pltpu.CompilerParams(vmem_limit_bytes=mib * 1024 * 1024)


def level_blocks(places, factors, chol, noise, got, out, section, half, after=()):
    depth, blocks, rows, _ = chol.shape
    slots = factors.shape[2]
    width = noise.shape[3] // HALVES
    sizes = [array.shape[0] for array in got]
    starts = [sum(sizes[:i]) for i in range(len(sizes))]
    n_got, first = len(sizes), section == 0
    carried = [] if out is None else [out]
    n_in = 3 + (not first) + n_got
    columns = pl.ds(half * width, width)

    def body(*refs):
        tbl, lower_all, draws_all = refs[:3]
        arrived = refs[n_in - n_got : n_in]
        latest, full, lower, draws, sems, *rest = refs[n_in + len(carried) + len(after) :]
        if not first:
            mats_all, (mats, held, got_sems) = refs[3], rest

        def fetches(b):
            moves = [
                pltpu.make_async_copy(lower_all.at[section, b], lower.at[b], sems.at[0, b]),
                pltpu.make_async_copy(
                    draws_all.at[section, b, :, columns], draws.at[b], sems.at[1, b]
                ),
            ]
            if not first:
                moves.append(
                    pltpu.make_async_copy(mats_all.at[section - 1, b], mats.at[b], sems.at[2, b])
                )
            return moves

        def gather(i):
            return pltpu.make_async_copy(
                arrived[i], held.at[pl.ds(starts[i], sizes[i])], got_sems.at[i]
            )

        def store(b):
            return pltpu.make_async_copy(
                latest.at[b], full.at[section, b, :, columns], sems.at[3, b]
            )

        for move in fetches(0):
            move.start()
        for i in range(n_got):
            gather(i).start()
        for b in range(1, blocks):
            for move in fetches(b):
                move.start()
        for i in range(n_got):
            gather(i).wait()
        for b in range(blocks):
            for move in fetches(b):
                move.wait()
            total = jnp.dot(lower[b], draws[b], preferred_element_type=jnp.float32)
            if not first:
                for j in range(slots):
                    place = tbl[b * slots + j]
                    parent = held[jnp.maximum(place, 0)]
                    parent = jnp.where(place >= 0, parent, jnp.zeros_like(parent))
                    total += jnp.dot(mats[b, j], parent, preferred_element_type=jnp.float32)
            latest[b] = total.astype(jnp.bfloat16)
            store(b).start()
        for b in range(blocks):
            store(b).wait()

    scratch = [
        pltpu.VMEM((blocks, rows, rows), jnp.bfloat16),
        pltpu.VMEM((blocks, rows, width), jnp.bfloat16),
        pltpu.SemaphoreType.DMA((4, blocks)),
    ]
    if not first:
        scratch += [
            pltpu.VMEM((blocks, slots, rows, rows), jnp.bfloat16),
            pltpu.VMEM((sum(sizes), rows, width), jnp.bfloat16),
            pltpu.SemaphoreType.DMA((n_got,)),
        ]
    return pl.pallas_call(
        body,
        in_specs=[pl.BlockSpec(memory_space=pltpu.SMEM)]
        + [ANY] * (n_in - 1 + len(carried) + len(after)),
        out_specs=[pl.BlockSpec(memory_space=pltpu.VMEM), ANY],
        out_shape=[
            jax.ShapeDtypeStruct((blocks, rows, width), jnp.bfloat16),
            jax.ShapeDtypeStruct(noise.shape, jnp.bfloat16),
        ],
        scratch_shapes=scratch,
        input_output_aliases={n_in: 1} if carried else {},
        compiler_params=params(56 if first else 48),
        cost_estimate=pl.CostEstimate(
            flops=2 * blocks * rows * rows * width, bytes_accessed=8_000_000, transcendentals=0
        ),
        name=f"level_{section}_{half}",
    )(places, chol, noise, *([] if first else [factors]), *got, *carried, *after)


def pick(table, held, group, name, after=()):
    blocks, rows, width = held[0][0].shape
    ks = sorted(set(group[0] + group[1]))
    same_slots, prior_slots = len(group[0]) * CAP, len(group[1]) * CAPX
    n_same, n_prior = COLS * bool(group[0]), COLS * bool(group[1])
    total = COLS * (same_slots + prior_slots)
    flat = [level[k] for level in held for k in ks]
    count, each, levels = len(flat), len(ks), len(held)

    def body(tbl, *refs):
        held = refs[:count]
        targets = refs[count + len(after) : -1]
        same, prior = targets[:n_same], targets[n_same:]
        sems = refs[-1]

        def slot_copy(slot, source):
            if slot < COLS * same_slots:
                target = same[slot // same_slots].at[slot % same_slots]
            else:
                left = slot - COLS * same_slots
                target = prior[left // prior_slots].at[left % prior_slots]
            return pltpu.make_async_copy(source, target, sems.at[slot])

        for slot in range(total):
            where = tbl[slot]
            if slot < COLS * same_slots:
                k = group[0][slot % same_slots // CAP]
            else:
                k = group[1][(slot - COLS * same_slots) % prior_slots // CAPX]
            at = ks.index(k)
            for level in range(levels):

                @pl.when((where >= level * blocks) & (where < (level + 1) * blocks))
                def _():
                    slot_copy(slot, held[level * each + at].at[where - level * blocks]).start()

        for slot in range(total):

            @pl.when(tbl[slot] >= 0)
            def _():
                slot_copy(slot, held[0].at[0]).wait()

    out = pl.pallas_call(
        body,
        in_specs=[pl.BlockSpec(memory_space=pltpu.SMEM)] + [ANY] * (count + len(after)),
        out_specs=[ANY] * (n_same + n_prior),
        out_shape=[jax.ShapeDtypeStruct((same_slots, rows, width), jnp.bfloat16)] * n_same
        + [jax.ShapeDtypeStruct((prior_slots, rows, width), jnp.bfloat16)] * n_prior,
        scratch_shapes=[pltpu.SemaphoreType.DMA((total,))],
        compiler_params=params(4),
        cost_estimate=pl.CostEstimate(flops=0, bytes_accessed=6_000_000, transcendentals=0),
        name=name,
    )(table, *flat, *after)
    return out[:n_same], out[n_same:]


def ranks(active, lane):
    count = lane.shape[-1]
    earlier = jnp.arange(count)[:, None] > jnp.arange(count)[None, :]
    alike = (lane[..., :, None] == lane[..., None, :]) & active[..., None, :] & earlier
    return jnp.sum(alike.astype(jnp.int32), axis=-1)


def tables(parents, total_blocks, local_blocks, peer_count, tile_count):
    sections = parents.shape[0]
    own_lane, own_tile = lax.axis_index("lvl"), lax.axis_index("tile")
    own_z, own_col = own_lane // COLS, own_lane % COLS
    mine = parents.reshape(sections, -1)
    onward = lax.ppermute(
        mine,
        "tile",
        [(t + 1, t) for t in range(tile_count - 1)],
    )
    onward = jnp.where(own_tile + 1 < tile_count, onward, -1)
    pair = jnp.stack([mine, onward])
    lists = jnp.stack([pair] + [lax.ppermute(pair, "lvl", across(k, peer_count)) for k in (1, 2, 3)])

    def decode(ids):
        clipped = jnp.maximum(ids, 0)
        level, block = clipped // total_blocks, clipped % total_blocks
        dev = block // local_blocks
        return ids >= 0, level, dev // peer_count, dev % peer_count, block % local_blocks

    valid, level, tile, lane, within = decode(lists)
    active = valid & (tile == own_tile) & (lane % COLS == own_col)
    rank = jnp.minimum(ranks(active, lane), CAP - 1)
    slot = ((own_z - lane // COLS) % 4) * CAP + rank
    hits = active[..., None] & (slot[..., None] == jnp.arange(4 * CAP))
    source = level * local_blocks + within
    table = jnp.sum(jnp.where(hits, source[..., None] + 1, 0), axis=-2) - 1
    table = table.reshape(COLS, 2, sections, 4, CAP).transpose(1, 2, 0, 3, 4)
    sends = []
    for same_ks, prior_ks in GROUPS:
        same = [table[0, :, c, k] for c in range(COLS) for k in same_ks]
        prior = [table[1, :, c, k, :1] for c in range(COLS) for k in prior_ks]
        sends.append(jnp.concatenate(same + prior, axis=1))

    valid, level, tile, lane, within = decode(mine)
    from_prior = (tile != own_tile).astype(jnp.int32)
    rank = jnp.minimum(ranks(valid, lane + peer_count * from_prior), CAP - 1)
    apart = (lane % COLS) ^ own_col
    ring = (own_z - lane // COLS) % 4
    place, base = jnp.zeros_like(lane), 0
    for same_ks, prior_ks in GROUPS:
        for at, k in enumerate(same_ks):
            slot = base + (apart * len(same_ks) + at) * CAP + rank
            place = jnp.where((ring == k) & (from_prior == 0), slot, place)
        base += COLS * len(same_ks) * CAP
        for at, k in enumerate(prior_ks):
            slot = base + (apart * len(prior_ks) + at) * CAPX
            place = jnp.where((ring == k) & (from_prior == 1), slot, place)
        base += COLS * len(prior_ks) * CAPX
    return sends, jnp.where(valid, place, -1)


def across(k, peer_count):
    return [(lane, lane ^ k) for lane in range(peer_count)]


def ring_z(latest, peer_count):
    links = [(lane, (lane + COLS) % peer_count) for lane in range(peer_count)]
    held = [latest]
    for _ in range(3):
        held.append(lax.ppermute(held[-1], "lvl", links))
    return held


def swap_plane(same, prior, peer_count, tile_count):
    got = list(same[:1])
    for k in range(1, len(same)):
        got.append(lax.ppermute(same[k], "lvl", across(k, peer_count)))
    for k in range(len(prior)):
        links = [
            (t * peer_count + a, (t + 1) * peer_count + b)
            for t in range(tile_count - 1)
            for a, b in across(k, peer_count)
        ]
        got.append(lax.ppermute(prior[k], ("tile", "lvl"), links))
    return got


def shards(parents, factors, chol, noise):
    peer_count = lax.axis_size("lvl")
    tile_count = lax.axis_size("tile")
    depth, local_blocks = chol.shape[:2]
    total_blocks = local_blocks * peer_count * tile_count
    sends, places = tables(parents, total_blocks, local_blocks, peer_count, tile_count)
    held = [[], []]

    def spread(latest, half):
        held[half].append(ring_z(latest, peer_count))
        return held[half][-1]

    def swap(section, half, after=()):
        got = []
        for group, ks in enumerate(GROUPS):
            same, prior = pick(
                sends[group][section], held[half], ks, f"pick_{section}_{half}_{group}", after
            )
            got += swap_plane(same, prior, peer_count, tile_count)
        return got

    args = factors, chol, noise
    lead, out = level_blocks(places[0], *args, [], None, 0, 0)
    ring = spread(lead, 0)
    lag, out = level_blocks(places[0], *args, [], out, 0, 1, [ring[1]])
    got = swap(0, 0, [lag])
    ring = spread(lag, 1)
    for section in range(1, depth):
        more = section + 1 < depth
        at = places[section - 1]
        lead, out = level_blocks(at, *args, got, out, section, 0, [ring[2]])
        lag_got = swap(section - 1, 1, [lead])
        ring = spread(lead, 0) if more else None
        lag, out = level_blocks(at, *args, lag_got, out, section, 1, [ring[2]] if more else ())
        if more:
            got = swap(section, 0, [lag])
            ring = spread(lag, 1)
    return out


def solution(mesh):
    placed = (
        P(None, ("tile", "lvl"), None),
        P(None, ("tile", "lvl"), None, None, None),
        P(None, ("tile", "lvl"), None, None),
        P(None, ("tile", "lvl"), None, None),
    )
    return jax.shard_map(
        shards,
        mesh=mesh,
        in_specs=placed,
        out_specs=P(None, ("tile", "lvl"), None, None),
        check_vma=False,
    )
```

```python
import functools

import jax
import jax.numpy as jnp
from jax import lax
from jax.experimental import pallas as pl
from jax.experimental.pallas import tpu as pltpu
from jax.sharding import PartitionSpec as P

CAP = 2
CAPX = 1
COLS = 4
GROUPS = (((0, 1), ()), ((2, 3), (0, 1, 2, 3)))
HALVES = 2
ANY = pl.BlockSpec(memory_space=pl.ANY)


def params(mib):
    return pltpu.CompilerParams(vmem_limit_bytes=mib * 1024 * 1024)


def level_blocks(places, factors, chol, noise, got, out, section, half, after=()):
    depth, blocks, rows, _ = chol.shape
    slots = factors.shape[2]
    width = noise.shape[3] // HALVES
    sizes = [array.shape[0] for array in got]
    starts = [sum(sizes[:i]) for i in range(len(sizes))]
    n_got, first = len(sizes), section == 0
    carried = [] if out is None else [out]
    n_in = 3 + (not first) + n_got
    columns = pl.ds(half * width, width)

    def body(*refs):
        tbl, lower_all, draws_all = refs[:3]
        arrived = refs[n_in - n_got : n_in]
        latest, full, lower, draws, sems, *rest = refs[n_in + len(carried) + len(after) :]
        if not first:
            mats_all, (mats, held, got_sems) = refs[3], rest

        def fetches(b):
            moves = [
                pltpu.make_async_copy(lower_all.at[section, b], lower.at[b], sems.at[0, b]),
                pltpu.make_async_copy(
                    draws_all.at[section, b, :, columns], draws.at[b], sems.at[1, b]
                ),
            ]
            if not first:
                moves.append(
                    pltpu.make_async_copy(mats_all.at[section - 1, b], mats.at[b], sems.at[2, b])
                )
            return moves

        def gather(i):
            return pltpu.make_async_copy(
                arrived[i], held.at[pl.ds(starts[i], sizes[i])], got_sems.at[i]
            )

        def store(b):
            return pltpu.make_async_copy(
                latest.at[b], full.at[section, b, :, columns], sems.at[3, b]
            )

        for move in fetches(0):
            move.start()
        for i in range(n_got):
            gather(i).start()
        for b in range(1, blocks):
            for move in fetches(b):
                move.start()
        for b in range(blocks):
            for move in fetches(b):
                move.wait()
            total = jnp.dot(lower[b], draws[b], preferred_element_type=jnp.float32)
            for i in range(n_got if b == 0 else 0):
                gather(i).wait()
            if not first:
                for j in range(slots):
                    place = tbl[b * slots + j]
                    parent = held[jnp.maximum(place, 0)]
                    parent = jnp.where(place >= 0, parent, jnp.zeros_like(parent))
                    total += jnp.dot(mats[b, j], parent, preferred_element_type=jnp.float32)
            latest[b] = total.astype(jnp.bfloat16)
            store(b).start()
        for b in range(blocks):
            store(b).wait()

    scratch = [
        pltpu.VMEM((blocks, rows, rows), jnp.bfloat16),
        pltpu.VMEM((blocks, rows, width), jnp.bfloat16),
        pltpu.SemaphoreType.DMA((4, blocks)),
    ]
    if not first:
        scratch += [
            pltpu.VMEM((blocks, slots, rows, rows), jnp.bfloat16),
            pltpu.VMEM((sum(sizes), rows, width), jnp.bfloat16),
            pltpu.SemaphoreType.DMA((n_got,)),
        ]
    return pl.pallas_call(
        body,
        in_specs=[pl.BlockSpec(memory_space=pltpu.SMEM)]
        + [ANY] * (n_in - 1 + len(carried) + len(after)),
        out_specs=[pl.BlockSpec(memory_space=pltpu.VMEM), ANY],
        out_shape=[
            jax.ShapeDtypeStruct((blocks, rows, width), jnp.bfloat16),
            jax.ShapeDtypeStruct(noise.shape, jnp.bfloat16),
        ],
        scratch_shapes=scratch,
        input_output_aliases={n_in: 1} if carried else {},
        compiler_params=params(56 if first else 48),
        cost_estimate=pl.CostEstimate(
            flops=2 * blocks * rows * rows * width, bytes_accessed=8_000_000, transcendentals=0
        ),
        name=f"level_{section}_{half}",
    )(places, chol, noise, *([] if first else [factors]), *got, *carried, *after)


def pick(table, held, group, name, after=()):
    blocks, rows, width = held[0][0].shape
    ks = sorted(set(group[0] + group[1]))
    same_slots, prior_slots = len(group[0]) * CAP, len(group[1]) * CAPX
    n_same, n_prior = COLS * bool(group[0]), COLS * bool(group[1])
    total = COLS * (same_slots + prior_slots)
    flat = [level[k] for level in held for k in ks]
    count, each, levels = len(flat), len(ks), len(held)

    def body(tbl, *refs):
        held = refs[:count]
        targets = refs[count + len(after) : -1]
        same, prior = targets[:n_same], targets[n_same:]
        sems = refs[-1]

        def slot_copy(slot, source):
            if slot < COLS * same_slots:
                target = same[slot // same_slots].at[slot % same_slots]
            else:
                left = slot - COLS * same_slots
                target = prior[left // prior_slots].at[left % prior_slots]
            return pltpu.make_async_copy(source, target, sems.at[slot])

        for slot in range(total):
            where = tbl[slot]
            if slot < COLS * same_slots:
                k = group[0][slot % same_slots // CAP]
            else:
                k = group[1][(slot - COLS * same_slots) % prior_slots // CAPX]
            at = ks.index(k)
            for level in range(levels):

                @pl.when((where >= level * blocks) & (where < (level + 1) * blocks))
                def _():
                    slot_copy(slot, held[level * each + at].at[where - level * blocks]).start()

        for slot in range(total):

            @pl.when(tbl[slot] >= 0)
            def _():
                slot_copy(slot, held[0].at[0]).wait()

    out = pl.pallas_call(
        body,
        in_specs=[pl.BlockSpec(memory_space=pltpu.SMEM)] + [ANY] * (count + len(after)),
        out_specs=[ANY] * (n_same + n_prior),
        out_shape=[jax.ShapeDtypeStruct((same_slots, rows, width), jnp.bfloat16)] * n_same
        + [jax.ShapeDtypeStruct((prior_slots, rows, width), jnp.bfloat16)] * n_prior,
        scratch_shapes=[pltpu.SemaphoreType.DMA((total,))],
        compiler_params=params(4),
        cost_estimate=pl.CostEstimate(flops=0, bytes_accessed=6_000_000, transcendentals=0),
        name=name,
    )(table, *flat, *after)
    return out[:n_same], out[n_same:]


def ranks(active, lane):
    count = lane.shape[-1]
    earlier = jnp.arange(count)[:, None] > jnp.arange(count)[None, :]
    alike = (lane[..., :, None] == lane[..., None, :]) & active[..., None, :] & earlier
    return jnp.sum(alike.astype(jnp.int32), axis=-1)


def tables(parents, total_blocks, local_blocks, peer_count, tile_count):
    sections = parents.shape[0]
    own_lane, own_tile = lax.axis_index("lvl"), lax.axis_index("tile")
    own_z, own_col = own_lane // COLS, own_lane % COLS
    mine = parents.reshape(sections, -1)
    onward = lax.ppermute(
        mine,
        "tile",
        [(t + 1, t) for t in range(tile_count - 1)],
    )
    onward = jnp.where(own_tile + 1 < tile_count, onward, -1)
    pair = jnp.stack([mine, onward])
    lists = jnp.stack([pair] + [lax.ppermute(pair, "lvl", across(k, peer_count)) for k in (1, 2, 3)])

    def decode(ids):
        clipped = jnp.maximum(ids, 0)
        level, block = clipped // total_blocks, clipped % total_blocks
        dev = block // local_blocks
        return ids >= 0, level, dev // peer_count, dev % peer_count, block % local_blocks

    valid, level, tile, lane, within = decode(lists)
    active = valid & (tile == own_tile) & (lane % COLS == own_col)
    rank = jnp.minimum(ranks(active, lane), CAP - 1)
    slot = ((own_z - lane // COLS) % 4) * CAP + rank
    hits = active[..., None] & (slot[..., None] == jnp.arange(4 * CAP))
    source = level * local_blocks + within
    table = jnp.sum(jnp.where(hits, source[..., None] + 1, 0), axis=-2) - 1
    table = table.reshape(COLS, 2, sections, 4, CAP).transpose(1, 2, 0, 3, 4)
    sends = []
    for same_ks, prior_ks in GROUPS:
        same = [table[0, :, c, k] for c in range(COLS) for k in same_ks]
        prior = [table[1, :, c, k, :1] for c in range(COLS) for k in prior_ks]
        sends.append(jnp.concatenate(same + prior, axis=1))

    valid, level, tile, lane, within = decode(mine)
    from_prior = (tile != own_tile).astype(jnp.int32)
    rank = jnp.minimum(ranks(valid, lane + peer_count * from_prior), CAP - 1)
    apart = (lane % COLS) ^ own_col
    ring = (own_z - lane // COLS) % 4
    place, base = jnp.zeros_like(lane), 0
    for same_ks, prior_ks in GROUPS:
        for at, k in enumerate(same_ks):
            slot = base + (apart * len(same_ks) + at) * CAP + rank
            place = jnp.where((ring == k) & (from_prior == 0), slot, place)
        base += COLS * len(same_ks) * CAP
        for at, k in enumerate(prior_ks):
            slot = base + (apart * len(prior_ks) + at) * CAPX
            place = jnp.where((ring == k) & (from_prior == 1), slot, place)
        base += COLS * len(prior_ks) * CAPX
    return sends, jnp.where(valid, place, -1)


def across(k, peer_count):
    return [(lane, lane ^ k) for lane in range(peer_count)]


def ring_z(latest, peer_count):
    links = [(lane, (lane + COLS) % peer_count) for lane in range(peer_count)]
    held = [latest]
    for _ in range(3):
        held.append(lax.ppermute(held[-1], "lvl", links))
    return held


def swap_plane(same, prior, peer_count, tile_count):
    got = list(same[:1])
    for k in range(1, len(same)):
        got.append(lax.ppermute(same[k], "lvl", across(k, peer_count)))
    for k in range(len(prior)):
        links = [
            (t * peer_count + a, (t + 1) * peer_count + b)
            for t in range(tile_count - 1)
            for a, b in across(k, peer_count)
        ]
        got.append(lax.ppermute(prior[k], ("tile", "lvl"), links))
    return got


def shards(parents, factors, chol, noise):
    peer_count = lax.axis_size("lvl")
    tile_count = lax.axis_size("tile")
    depth, local_blocks = chol.shape[:2]
    total_blocks = local_blocks * peer_count * tile_count
    sends, places = tables(parents, total_blocks, local_blocks, peer_count, tile_count)
    held = [[], []]

    def spread(latest, half):
        held[half].append(ring_z(latest, peer_count))
        return held[half][-1]

    def swap(section, half, after=()):
        got = []
        for group, ks in enumerate(GROUPS):
            same, prior = pick(
                sends[group][section], held[half], ks, f"pick_{section}_{half}_{group}", after
            )
            got += swap_plane(same, prior, peer_count, tile_count)
        return got

    args = factors, chol, noise
    lead, out = level_blocks(places[0], *args, [], None, 0, 0)
    ring = spread(lead, 0)
    lag, out = level_blocks(places[0], *args, [], out, 0, 1, [ring[1]])
    got = swap(0, 0, [lag])
    ring = spread(lag, 1)
    for section in range(1, depth):
        more = section + 1 < depth
        at = places[section - 1]
        lead, out = level_blocks(at, *args, got, out, section, 0, [ring[2]])
        lag_got = swap(section - 1, 1, [lead])
        ring = spread(lead, 0) if more else None
        lag, out = level_blocks(at, *args, lag_got, out, section, 1, [ring[2]] if more else ())
        if more:
            got = swap(section, 0, [lag])
            ring = spread(lag, 1)
    return out


def solution(mesh):
    placed = (
        P(None, ("tile", "lvl"), None),
        P(None, ("tile", "lvl"), None, None, None),
        P(None, ("tile", "lvl"), None, None),
        P(None, ("tile", "lvl"), None, None),
    )
    return jax.shard_map(
        shards,
        mesh=mesh,
        in_specs=placed,
        out_specs=P(None, ("tile", "lvl"), None, None),
        check_vma=False,
    )
```

```python
import functools

import jax
import jax.numpy as jnp
from jax import lax
from jax.experimental import pallas as pl
from jax.experimental.pallas import tpu as pltpu
from jax.sharding import PartitionSpec as P

CAP = 2
CAPX = 1
COLS = 4
GROUPS = (((0, 1), ()), ((2, 3), (0, 1, 2, 3)))
HALVES = 2
ANY = pl.BlockSpec(memory_space=pl.ANY)


def params(mib):
    return pltpu.CompilerParams(vmem_limit_bytes=mib * 1024 * 1024)


def level_blocks(places, factors, chol, noise, got, out, section, half, after=()):
    depth, blocks, rows, _ = chol.shape
    slots = factors.shape[2]
    width = noise.shape[3] // HALVES
    sizes = [array.shape[0] for array in got]
    starts = [sum(sizes[:i]) for i in range(len(sizes))]
    n_got, first = len(sizes), section == 0
    carried = [] if out is None else [out]
    n_in = 3 + (not first) + n_got
    columns = pl.ds(half * width, width)

    def body(*refs):
        tbl, lower_all, draws_all = refs[:3]
        arrived = refs[n_in - n_got : n_in]
        latest, full, lower, draws, sems, *rest = refs[n_in + len(carried) + len(after) :]
        if not first:
            mats_all, (mats, held, got_sems) = refs[3], rest

        def fetches(b):
            moves = [
                pltpu.make_async_copy(lower_all.at[section, b], lower.at[b], sems.at[0, b]),
                pltpu.make_async_copy(
                    draws_all.at[section, b, :, columns], draws.at[b], sems.at[1, b]
                ),
            ]
            if not first:
                moves.append(
                    pltpu.make_async_copy(mats_all.at[section - 1, b], mats.at[b], sems.at[2, b])
                )
            return moves

        def gather(i):
            return pltpu.make_async_copy(
                arrived[i], held.at[pl.ds(starts[i], sizes[i])], got_sems.at[i]
            )

        def store(b):
            return pltpu.make_async_copy(
                latest.at[b], full.at[section, b, :, columns], sems.at[3, b]
            )

        for move in fetches(0):
            move.start()
        for i in range(n_got):
            gather(i).start()
        for b in range(1, blocks):
            for move in fetches(b):
                move.start()
        for i in range(n_got):
            gather(i).wait()
        for b in range(blocks):
            for move in fetches(b):
                move.wait()
            total = jnp.dot(lower[b], draws[b], preferred_element_type=jnp.float32)
            if not first:
                for j in range(slots):
                    place = tbl[b * slots + j]
                    parent = held[jnp.maximum(place, 0)]
                    parent = jnp.where(place >= 0, parent, jnp.zeros_like(parent))
                    total += jnp.dot(mats[b, j], parent, preferred_element_type=jnp.float32)
            latest[b] = total.astype(jnp.bfloat16)
            store(b).start()
        for b in range(blocks):
            store(b).wait()

    scratch = [
        pltpu.VMEM((blocks, rows, rows), jnp.bfloat16),
        pltpu.VMEM((blocks, rows, width), jnp.bfloat16),
        pltpu.SemaphoreType.DMA((4, blocks)),
    ]
    if not first:
        scratch += [
            pltpu.VMEM((blocks, slots, rows, rows), jnp.bfloat16),
            pltpu.VMEM((sum(sizes), rows, width), jnp.bfloat16),
            pltpu.SemaphoreType.DMA((n_got,)),
        ]
    return pl.pallas_call(
        body,
        in_specs=[pl.BlockSpec(memory_space=pltpu.SMEM)]
        + [ANY] * (n_in - 1 + len(carried) + len(after)),
        out_specs=[pl.BlockSpec(memory_space=pltpu.VMEM), ANY],
        out_shape=[
            jax.ShapeDtypeStruct((blocks, rows, width), jnp.bfloat16),
            jax.ShapeDtypeStruct(noise.shape, jnp.bfloat16),
        ],
        scratch_shapes=scratch,
        input_output_aliases={n_in: 1} if carried else {},
        compiler_params=params(56 if first else 48),
        cost_estimate=pl.CostEstimate(
            flops=2 * blocks * rows * rows * width, bytes_accessed=8_000_000, transcendentals=0
        ),
        name=f"level_{section}_{half}",
    )(places, chol, noise, *([] if first else [factors]), *got, *carried, *after)


def pick(table, held, group, name, after=()):
    blocks, rows, width = held[0][0].shape
    ks = sorted(set(group[0] + group[1]))
    same_slots, prior_slots = len(group[0]) * CAP, len(group[1]) * CAPX
    n_same, n_prior = COLS * bool(group[0]), COLS * bool(group[1])
    total = COLS * (same_slots + prior_slots)
    flat = [level[k] for level in held for k in ks]
    count, each, levels = len(flat), len(ks), len(held)

    def body(tbl, *refs):
        held = refs[:count]
        targets = refs[count + len(after) : -1]
        same, prior = targets[:n_same], targets[n_same:]
        sems = refs[-1]

        def slot_copy(slot, source):
            if slot < COLS * same_slots:
                target = same[slot // same_slots].at[slot % same_slots]
            else:
                left = slot - COLS * same_slots
                target = prior[left // prior_slots].at[left % prior_slots]
            return pltpu.make_async_copy(source, target, sems.at[slot])

        for slot in range(total):
            where = tbl[slot]
            if slot < COLS * same_slots:
                k = group[0][slot % same_slots // CAP]
            else:
                k = group[1][(slot - COLS * same_slots) % prior_slots // CAPX]
            at = ks.index(k)
            for level in range(levels):

                @pl.when((where >= level * blocks) & (where < (level + 1) * blocks))
                def _():
                    slot_copy(slot, held[level * each + at].at[where - level * blocks]).start()

        for slot in range(total):

            @pl.when(tbl[slot] >= 0)
            def _():
                slot_copy(slot, held[0].at[0]).wait()

    out = pl.pallas_call(
        body,
        in_specs=[pl.BlockSpec(memory_space=pltpu.SMEM)] + [ANY] * (count + len(after)),
        out_specs=[ANY] * (n_same + n_prior),
        out_shape=[jax.ShapeDtypeStruct((same_slots, rows, width), jnp.bfloat16)] * n_same
        + [jax.ShapeDtypeStruct((prior_slots, rows, width), jnp.bfloat16)] * n_prior,
        scratch_shapes=[pltpu.SemaphoreType.DMA((total,))],
        compiler_params=params(1),
        cost_estimate=pl.CostEstimate(flops=0, bytes_accessed=6_000_000, transcendentals=0),
        name=name,
    )(table, *flat, *after)
    return out[:n_same], out[n_same:]


def ranks(active, lane):
    count = lane.shape[-1]
    earlier = jnp.arange(count)[:, None] > jnp.arange(count)[None, :]
    alike = (lane[..., :, None] == lane[..., None, :]) & active[..., None, :] & earlier
    return jnp.sum(alike.astype(jnp.int32), axis=-1)


def tables(parents, total_blocks, local_blocks, peer_count, tile_count):
    sections = parents.shape[0]
    own_lane, own_tile = lax.axis_index("lvl"), lax.axis_index("tile")
    own_z, own_col = own_lane // COLS, own_lane % COLS
    mine = parents.reshape(sections, -1)
    onward = lax.ppermute(
        mine,
        "tile",
        [(t + 1, t) for t in range(tile_count - 1)],
    )
    onward = jnp.where(own_tile + 1 < tile_count, onward, -1)
    pair = jnp.stack([mine, onward])
    lists = jnp.stack([pair] + [lax.ppermute(pair, "lvl", across(k, peer_count)) for k in (1, 2, 3)])

    def decode(ids):
        clipped = jnp.maximum(ids, 0)
        level, block = clipped // total_blocks, clipped % total_blocks
        dev = block // local_blocks
        return ids >= 0, level, dev // peer_count, dev % peer_count, block % local_blocks

    valid, level, tile, lane, within = decode(lists)
    active = valid & (tile == own_tile) & (lane % COLS == own_col)
    rank = jnp.minimum(ranks(active, lane), CAP - 1)
    slot = ((own_z - lane // COLS) % 4) * CAP + rank
    hits = active[..., None] & (slot[..., None] == jnp.arange(4 * CAP))
    source = level * local_blocks + within
    table = jnp.sum(jnp.where(hits, source[..., None] + 1, 0), axis=-2) - 1
    table = table.reshape(COLS, 2, sections, 4, CAP).transpose(1, 2, 0, 3, 4)
    sends = []
    for same_ks, prior_ks in GROUPS:
        same = [table[0, :, c, k] for c in range(COLS) for k in same_ks]
        prior = [table[1, :, c, k, :1] for c in range(COLS) for k in prior_ks]
        sends.append(jnp.concatenate(same + prior, axis=1))

    valid, level, tile, lane, within = decode(mine)
    from_prior = (tile != own_tile).astype(jnp.int32)
    rank = jnp.minimum(ranks(valid, lane + peer_count * from_prior), CAP - 1)
    apart = (lane % COLS) ^ own_col
    ring = (own_z - lane // COLS) % 4
    place, base = jnp.zeros_like(lane), 0
    for same_ks, prior_ks in GROUPS:
        for at, k in enumerate(same_ks):
            slot = base + (apart * len(same_ks) + at) * CAP + rank
            place = jnp.where((ring == k) & (from_prior == 0), slot, place)
        base += COLS * len(same_ks) * CAP
        for at, k in enumerate(prior_ks):
            slot = base + (apart * len(prior_ks) + at) * CAPX
            place = jnp.where((ring == k) & (from_prior == 1), slot, place)
        base += COLS * len(prior_ks) * CAPX
    return sends, jnp.where(valid, place, -1)


def across(k, peer_count):
    return [(lane, lane ^ k) for lane in range(peer_count)]


def ring_z(latest, peer_count):
    links = [(lane, (lane + COLS) % peer_count) for lane in range(peer_count)]
    held = [latest]
    for _ in range(3):
        held.append(lax.ppermute(held[-1], "lvl", links))
    return held


def swap_plane(same, prior, peer_count, tile_count):
    got = list(same[:1])
    for k in range(1, len(same)):
        got.append(lax.ppermute(same[k], "lvl", across(k, peer_count)))
    for k in range(len(prior)):
        links = [
            (t * peer_count + a, (t + 1) * peer_count + b)
            for t in range(tile_count - 1)
            for a, b in across(k, peer_count)
        ]
        got.append(lax.ppermute(prior[k], ("tile", "lvl"), links))
    return got


def shards(parents, factors, chol, noise):
    peer_count = lax.axis_size("lvl")
    tile_count = lax.axis_size("tile")
    depth, local_blocks = chol.shape[:2]
    total_blocks = local_blocks * peer_count * tile_count
    sends, places = tables(parents, total_blocks, local_blocks, peer_count, tile_count)
    held = [[], []]

    def spread(latest, half):
        held[half].append(ring_z(latest, peer_count))
        return held[half][-1]

    def swap(section, half, after=()):
        got = []
        for group, ks in enumerate(GROUPS):
            same, prior = pick(
                sends[group][section], held[half], ks, f"pick_{section}_{half}_{group}", after
            )
            got += swap_plane(same, prior, peer_count, tile_count)
        return got

    args = factors, chol, noise
    lead, out = level_blocks(places[0], *args, [], None, 0, 0)
    ring = spread(lead, 0)
    lag, out = level_blocks(places[0], *args, [], out, 0, 1, [ring[1]])
    got = swap(0, 0, [lag])
    ring = spread(lag, 1)
    for section in range(1, depth):
        more = section + 1 < depth
        at = places[section - 1]
        lead, out = level_blocks(at, *args, got, out, section, 0, [ring[2]])
        lag_got = swap(section - 1, 1, [lead])
        ring = spread(lead, 0) if more else None
        lag, out = level_blocks(at, *args, lag_got, out, section, 1, [ring[2]] if more else ())
        if more:
            got = swap(section, 0, [lag])
            ring = spread(lag, 1)
    return out


def solution(mesh):
    placed = (
        P(None, ("tile", "lvl"), None),
        P(None, ("tile", "lvl"), None, None, None),
        P(None, ("tile", "lvl"), None, None),
        P(None, ("tile", "lvl"), None, None),
    )
    return jax.shard_map(
        shards,
        mesh=mesh,
        in_specs=placed,
        out_specs=P(None, ("tile", "lvl"), None, None),
        check_vma=False,
    )
```
